32 devices in a mesh: dp: 16 (over z, y, x), factor: 2 (over core).
Axes of the slice: x: 2, y: 2, z: 4, core: 2. Of those that a mesh axis runs over, the one named last changes fastest.
Arguments:
- layer_inputs: bfloat16 [16384, 5120], P('dp', 'factor'), may hold values from -64 to 64
- out_grads: bfloat16 [16384, 5120], P('dp', 'factor'), may hold values from -64 to 64
- weight_grad: bfloat16 [5120, 5120], P('dp', 'factor'), may hold values from -32 to 32
- left_inv: float32 [5120, 5120], P('dp', 'factor'), may hold values from -4 to 10, as said below
- right_inv: float32 [5120, 5120], P('factor', 'dp'), may hold values from -4 to 10, as said below
Outputs:
- precond_grad: bfloat16 [5120, 5120], P('dp', 'factor')
- new_left: float32 [5120, 5120], P('dp', 'factor')
- new_right: float32 [5120, 5120], P('factor', 'dp')
The draws below stay inside these ranges and needn't reach their ends.
Inputs may be any that keep to these rules, and one draw needn't show every extreme that they name: `left_inv`: symmetric and positive definite, every eigenvalue 0.1 or more. `right_inv`: symmetric and positive definite, every eigenvalue 0.1 or more.
All inputs are finite; a program needn't handle non-finite values.
Results may differ from the reference program's by a relative error of at most 0.00275.
The reference program's roundings to bfloat16 on the way (of `hidden`) count: a program that leaves them out, or rounds other values in their place, can miss the bound.
Values may be sent and summed in bfloat16 or wider, within the bound.
A program may use at most 128 MiB of HBM per device.

```python
import math
import jax
import jax.numpy as jnp
from jax import lax

D = 5120
TOK_DEV = 1024
TOKENS = 16384


def column_ramp_values():
    return jnp.exp(jnp.arange(D, dtype=jnp.float32) / max(D - 1, 1) * math.log(10.0))


def mean_dirs(key):
    key_amag, key_asign, key_gmag, key_gsign = jax.random.split(jax.random.fold_in(key, 4021), 4)
    column_ramp = column_ramp_values()
    act_mag = jnp.exp(jax.random.uniform(key_amag, (D,), jnp.float32, math.log(0.1), math.log(1.0)))
    grad_mag = jnp.exp(jax.random.uniform(key_gmag, (D,), jnp.float32, math.log(0.1), math.log(1.0)))
    act_centre = jax.random.rademacher(key_asign, (D,), dtype=jnp.float32) * act_mag * column_ramp
    grad_centre = jax.random.rademacher(key_gsign, (D,), dtype=jnp.float32) * grad_mag * column_ramp
    return (act_centre, grad_centre)


def token_rows(key, centre):
    key_noise, key_omag, key_osign = jax.random.split(key, 3)
    block_count = TOKENS // TOK_DEV
    column_ramp = column_ramp_values()
    offset_mag = jnp.exp(jax.random.uniform(key_omag, (block_count, D), jnp.float32, math.log(0.1), math.log(1.0)))
    offsets = jax.random.rademacher(key_osign, (block_count, D), dtype=jnp.float32) * offset_mag * column_ramp[None, :]
    row_offsets = jnp.repeat(offsets, TOK_DEV, axis=0, total_repeat_length=TOKENS)
    position = jnp.arange(TOKENS, dtype=jnp.float32) / max(TOKENS - 1, 1)
    row_scale = jnp.exp(position * math.log(3.0))
    noise = jnp.clip(jax.random.normal(key_noise, (TOKENS, D), jnp.float32), -5.0, 5.0)
    return jnp.clip(row_scale[:, None] * (centre[None, :] + row_offsets + noise), -64.0, 64.0)


def draw_layer_inputs(key, part):
    act_centre, grad_centre = mean_dirs(key)
    return token_rows(jax.random.fold_in(key, 31), act_centre).astype(jnp.bfloat16)


def draw_out_grads(key, part):
    act_centre, grad_centre = mean_dirs(key)
    return token_rows(jax.random.fold_in(key, 37), grad_centre).astype(jnp.bfloat16)


def draw_weight_grad(key, part):
    act_centre, grad_centre = mean_dirs(key)
    key_left, key_right, key_noise = jax.random.split(jax.random.fold_in(key, 41), 3)
    left_dir = act_centre / jnp.sqrt(jnp.mean(act_centre * act_centre))
    right_dir = grad_centre / jnp.sqrt(jnp.mean(grad_centre * grad_centre))
    left_mix = jnp.clip(jax.random.normal(key_left, (D,), jnp.float32), -4.0, 4.0)
    right_mix = jnp.clip(jax.random.normal(key_right, (D,), jnp.float32), -4.0, 4.0)
    noise = 0.25 * jnp.clip(jax.random.normal(key_noise, (D, D), jnp.float32), -5.0, 5.0)
    full = noise + left_dir[:, None] * left_mix[None, :] + right_mix[:, None] * right_dir[None, :]
    return jnp.clip(full, -32.0, 32.0).astype(jnp.bfloat16)


def definite(key):
    key_base = jax.random.fold_in(key, 0)
    base = jax.random.normal(key_base, (D, D), jnp.float32)
    product = jnp.dot(base, base.T, precision=lax.Precision.HIGHEST) / D
    matrix = 0.5 * jnp.eye(D, dtype=jnp.float32) + 0.5 * (product + product.T)
    return jnp.clip(matrix, -4.0, 10.0)


def draw_left_inv(key, part):
    return definite(jax.random.fold_in(key, 13))


def draw_right_inv(key, part):
    return definite(jax.random.fold_in(key, 17))


def setup_inputs(seed: int = 0) -> dict:
    seeds = jax.random.split(jax.random.key(seed), 6)
    layer_inputs = draw_layer_inputs(jax.random.fold_in(seeds[5], 71), 0)
    out_grads = draw_out_grads(jax.random.fold_in(seeds[5], 71), 0)
    weight_grad = draw_weight_grad(jax.random.fold_in(seeds[5], 71), 0)
    left_inv = draw_left_inv(jax.random.fold_in(seeds[5], 71), 0)
    right_inv = draw_right_inv(jax.random.fold_in(seeds[5], 71), 0)
    return {"layer_inputs": layer_inputs, "out_grads": out_grads, "weight_grad": weight_grad, "left_inv": left_inv, "right_inv": right_inv}


decay = 0.9


def coefficient(quadratic):
    return (1.0 - decay) / (decay * decay * (1.0 + (1.0 - decay) / decay * quadratic))


def reference(layer_inputs, out_grads, weight_grad, left_inv, right_inv):
    token_count = layer_inputs.shape[0]
    mean_act = jnp.sum(layer_inputs, axis=0, dtype=jnp.float32) / token_count
    mean_grad = jnp.sum(out_grads, axis=0, dtype=jnp.float32) / token_count
    left_image = jnp.dot(left_inv, mean_act, precision=lax.Precision.HIGHEST)
    right_image = jnp.dot(right_inv, mean_grad, precision=lax.Precision.HIGHEST)
    left_quad = jnp.sum(mean_act * left_image)
    right_quad = jnp.sum(mean_grad * right_image)
    left_coef = coefficient(left_quad)
    right_coef = coefficient(right_quad)
    new_left = left_inv / decay - left_coef * left_image[:, None] * left_image[None, :]
    new_right = right_inv / decay - right_coef * right_image[:, None] * right_image[None, :]
    left_half = new_left.astype(jnp.bfloat16)
    right_half = new_right.astype(jnp.bfloat16)
    hidden = jnp.dot(left_half, weight_grad, preferred_element_type=jnp.float32).astype(jnp.bfloat16)
    precond_grad = jnp.dot(hidden, right_half, preferred_element_type=jnp.float32).astype(jnp.bfloat16)
    return precond_grad, new_left, new_right
```

```python
import functools
import jax
import jax.numpy as jnp
from jax import lax
from jax.experimental import pallas as pl
from jax.experimental.pallas import tpu as pltpu
from jax.sharding import PartitionSpec as P

decay = 0.9


def coefficient(quadratic):
    return (1.0 - decay) / (decay * decay * (1.0 + (1.0 - decay) / decay * quadratic))


def gathered(layer_inputs, out_grads, weight_grad, left_inv, right_inv):
    highest = lax.Precision.HIGHEST
    token_count = layer_inputs.shape[0] * lax.axis_size("dp")
    act_local = jnp.sum(layer_inputs, axis=0, dtype=jnp.float32)
    grad_local = jnp.sum(out_grads, axis=0, dtype=jnp.float32)
    act_sums, grad_sums = lax.psum((act_local, grad_local), "dp")
    mean_act = act_sums / token_count
    mean_grad = grad_sums / token_count
    whole_act, whole_grad = (
        lax.all_gather(mean_act, "factor", axis=0, tiled=True),
        lax.all_gather(mean_grad, "factor", axis=0, tiled=True),
    )
    left_rows, left_cols = left_inv.shape
    right_rows, right_cols = right_inv.shape
    data_index = lax.axis_index("dp")
    act_rows = lax.dynamic_slice_in_dim(whole_act, data_index * left_rows, left_rows)
    grad_cols = lax.dynamic_slice_in_dim(whole_grad, data_index * right_cols, right_cols)
    row_terms = jnp.dot(left_inv, mean_act, precision=highest)
    col_terms = jnp.dot(mean_grad, right_inv, precision=highest)
    left_image_rows, right_image_cols = lax.psum((row_terms, col_terms), "factor")
    left_partial = jnp.dot(act_rows, left_inv, precision=highest)
    right_partial = jnp.dot(right_inv, grad_cols, precision=highest)
    left_image_cols, right_image_rows = lax.psum((left_partial, right_partial), "dp")
    left_quad, right_quad = lax.psum(
        (jnp.sum(mean_act * left_image_cols), jnp.sum(mean_grad * right_image_rows)), "factor"
    )
    left_coef = coefficient(left_quad)
    right_coef = coefficient(right_quad)
    new_left = left_inv / decay - left_coef * left_image_rows[:, None] * left_image_cols[None, :]
    new_right = (
        right_inv / decay - right_coef * right_image_rows[:, None] * right_image_cols[None, :]
    )
    left_half = new_left.astype(jnp.bfloat16)
    right_half = new_right.astype(jnp.bfloat16)
    left_wide = lax.all_gather(left_half, "factor", axis=1, tiled=True)
    matched = left_wide
    hidden_sum = jnp.dot(
        matched,
        lax.all_gather(weight_grad, "dp", axis=0, tiled=True),
        preferred_element_type=jnp.float32,
    )
    hidden = hidden_sum.astype(jnp.bfloat16)
    hidden_wide = lax.all_gather(hidden, "factor", axis=1, tiled=True)
    matched = hidden_wide
    precond = lax.dot_general(
        matched,
        lax.all_gather(right_half, "dp", axis=1, tiled=True),
        (((1,), (1,)), ((), ())),
        preferred_element_type=jnp.float32,
    )
    return (precond.astype(jnp.bfloat16), new_left, new_right)


MESH = pl.DeviceIdType.MESH


def split(count):
    inner = 1
    for size in range(1, count + 1):
        if count % size == 0 and size * size <= count:
            inner = size
    return count // inner, inner


def kernel(
    outer, inner, cores, tokens,
    sums_ref, w_ref, l_ref, r_ref,
    out_ref, new_l_ref, new_r_ref,
    sums_all, mean_all, part_all, image, image_half, columns,
    l_buf, r_buf, r_half, w_panel, l_panel, r_panel, h_panel, result,
    load_sem, store_sem,
    sums_send, mean_send, part_send, w_send, l_send, r_send, h_send, out_send,
    sums_recv, mean_recv, part_recv, w_recv, l_recv, r_recv, h_recv, out_recv,
):
    data = outer * inner
    count = data * cores
    plane = inner * cores
    rows, cols = l_buf.shape
    width = w_panel.shape[1]
    me_data = lax.axis_index("dp")
    me_core = lax.axis_index("factor")
    me = me_data * cores + me_core
    me_outer = me_data // inner
    me_inner = me_data % inner

    def remote(src, dst, send, recv, target_data, target_core):
        return pltpu.make_async_remote_copy(
            src_ref=src, dst_ref=dst, send_sem=send, recv_sem=recv,
            device_id=(target_data, target_core), device_id_type=MESH,
        )

    def each(total, body):
        def step(index, carry):
            body(index)
            return carry

        lax.fori_loop(0, total, step, 0)

    load_l = pltpu.make_async_copy(l_ref, l_buf, load_sem.at[0])
    load_r = pltpu.make_async_copy(r_ref, r_buf, load_sem.at[1])
    load_l.start()
    load_r.start()
    sums_all[me_data] = sums_ref[...]

    barrier = pltpu.get_barrier_semaphore()

    def greet(index):
        target = (me + 1 + index) % count
        pl.semaphore_signal(
            barrier, inc=1, device_id=(target // cores, target % cores), device_id_type=MESH
        )

    each(count - 1, greet)
    pl.semaphore_wait(barrier, count - 1)

    def sums_copy(index):
        target = (me_data + 1 + index) % data
        return remote(
            sums_all.at[me_data], sums_all.at[me_data],
            sums_send.at[index], sums_recv, target, me_core,
        )

    each(data - 1, lambda index: sums_copy(index).start())

    def w_copy(index):
        target = (me_data + 1 + index) % data
        return remote(
            w_ref.at[:, pl.ds(pl.multiple_of((target % inner) * width, width), width)],
            w_panel.at[pl.ds(pl.multiple_of(me_data * rows, rows), rows), :],
            w_send.at[index], w_recv, target, me_core,
        )

    w_own = pltpu.make_async_copy(
        w_ref.at[:, pl.ds(pl.multiple_of(me_inner * width, width), width)],
        w_panel.at[pl.ds(pl.multiple_of(me_data * rows, rows), rows), :],
        w_recv,
    )

    def start_w():
        each(data - 1, lambda index: w_copy(index).start())
        w_own.start()

    start_w()

    some = sums_all.at[pl.ds(0, data - 1)]
    pltpu.make_async_copy(some, some, sums_recv).wait()
    mean = jnp.sum(sums_all[...], axis=0) / tokens
    mean_all[me_core] = mean

    def mean_copy(index):
        target = (me_core + 1 + index) % cores
        return remote(
            mean_all.at[me_core], mean_all.at[me_core],
            mean_send.at[index], mean_recv, me_data, target,
        )

    each(cores - 1, lambda index: mean_copy(index).start())
    load_l.wait()
    load_r.wait()
    step = 32
    for side, buf in enumerate((l_buf, r_buf)):

        def partial(index, side=side, buf=buf):
            piece = pl.ds(pl.multiple_of(index * step, step), step)
            total = jnp.sum(
                buf[piece, :] * mean_all[me_core][side : side + 1, :], axis=1, keepdims=True
            )
            columns[side, piece, :] = jnp.broadcast_to(total, (step, 128))

        each(rows // step, partial)
    part_all[me] = jnp.concatenate(
        [jnp.transpose(columns[side])[0:1, :] for side in range(2)], axis=0
    )

    def part_copy(index):
        target = (me + 1 + index) % count
        return remote(
            part_all.at[me], part_all.at[me],
            part_send.at[index], part_recv, target // cores, target % cores,
        )

    each(count - 1, lambda index: part_copy(index).start())

    other_means = mean_all.at[pl.ds(0, cores - 1)]
    pltpu.make_async_copy(other_means, other_means, mean_recv).wait()
    other_parts = part_all.at[pl.ds(0, count - 1)]
    pltpu.make_async_copy(other_parts, other_parts, part_recv).wait()

    per_core = data // cores
    quad = jnp.zeros((2, 1), jnp.float32)
    for core in range(cores):
        blocks = []
        for block in range(core * per_core, (core + 1) * per_core):
            total = part_all[block * cores]
            for other in range(1, cores):
                total = total + part_all[block * cores + other]
            image[block] = total
            blocks.append(total)
        half = jnp.concatenate(blocks, axis=1)
        image_half[core] = half
        quad = quad + jnp.sum(mean_all[core] * half, axis=1, keepdims=True)
    coef = (1.0 - decay) / (decay * decay * (1.0 + (1.0 - decay) / decay * quad))
    scaled = image[me_data] * coef
    for side in range(2):
        columns[side] = jnp.transpose(jnp.broadcast_to(scaled[side : side + 1, :], (128, rows)))

    for side, buf in enumerate((l_buf, r_buf)):

        def update(index, side=side, buf=buf):
            piece = pl.ds(pl.multiple_of(index * step, step), step)
            fresh = buf[piece, :] * (1.0 / decay) - (
                columns[side, piece, :][:, 0:1] * image_half[me_core][side : side + 1, :]
            )
            buf[piece, :] = fresh
            if side == 0:
                l_panel[
                    pl.ds(pl.multiple_of(me_inner * rows + index * step, step), step),
                    pl.ds(pl.multiple_of(me_core * cols, cols), cols),
                ] = fresh.astype(jnp.bfloat16)
            else:
                r_half[piece, :] = fresh.astype(jnp.bfloat16)

        each(rows // step, update)

    store_l = pltpu.make_async_copy(l_buf, new_l_ref, store_sem.at[0])
    store_r = pltpu.make_async_copy(r_buf, new_r_ref, store_sem.at[1])
    store_l.start()
    store_r.start()

    l_own = l_panel.at[
        pl.ds(pl.multiple_of(me_inner * rows, rows), rows),
        pl.ds(pl.multiple_of(me_core * cols, cols), cols),
    ]
    me_plane = me_inner * cores + me_core

    def neighbour(index):
        target = (me_plane + 1 + index) % plane
        return me_outer * inner + target // cores, target % cores

    def l_copy(index):
        return remote(l_own, l_own, l_send.at[index], l_recv, *neighbour(index))

    each(plane - 1, lambda index: l_copy(index).start())

    slots = outer // cores
    r_core = me_data // per_core
    r_inner = (me_data % per_core) // slots
    r_slot = me_data % slots
    r_target = r_panel.at[
        pl.ds(pl.multiple_of(r_slot * rows, rows), rows),
        pl.ds(pl.multiple_of(me_core * cols, cols), cols),
    ]
    keeps = jnp.logical_and(r_core == me_core, r_inner == me_inner)
    r_local = pltpu.make_async_copy(r_half, r_target, r_recv)

    def r_copy(index):
        target = (me_outer + 1 + index) % outer
        return remote(
            r_half, r_target, r_send.at[index], r_recv, target * inner + r_inner, r_core
        )

    each(outer - 1, lambda index: r_copy(index).start())

    @pl.when(keeps)
    def _():
        r_local.start()

    @pl.when(jnp.logical_not(keeps))
    def _():
        r_copy(outer - 1).start()

    pltpu.make_async_copy(w_panel, w_panel, w_recv).wait()
    other_l = l_panel.at[pl.ds(0, (plane - 1) * rows // cores), :]
    pltpu.make_async_copy(other_l, other_l, l_recv).wait()

    h_columns = pl.ds(pl.multiple_of(me_core * cols + me_inner * width, width), width)

    def first(index):
        piece = pl.ds(pl.multiple_of(index * rows, rows), rows)
        h_panel[piece, h_columns] = jnp.dot(
            l_panel[piece, :], w_panel[...], preferred_element_type=jnp.float32
        ).astype(jnp.bfloat16)

    each(inner, first)

    h_own = h_panel.at[:, h_columns]

    def h_copy(index):
        return remote(h_own, h_own, h_send.at[index], h_recv, *neighbour(index))

    each(plane - 1, lambda index: h_copy(index).start())

    pltpu.make_async_copy(r_panel, r_panel, r_recv).wait()
    other_h = h_panel.at[:, pl.ds(0, (plane - 1) * width)]
    pltpu.make_async_copy(other_h, other_h, h_recv).wait()

    out_columns = out_ref.at[:, pl.ds(pl.multiple_of(me_inner * width, width), width)]

    def out_copy(index):
        target = (me_inner + 1 + index) % inner
        return remote(
            result.at[pl.ds(pl.multiple_of(target * rows, rows), rows), :], out_columns,
            out_send.at[index], out_recv, me_outer * inner + target, me_core,
        )

    out_own = pltpu.make_async_copy(
        result.at[pl.ds(pl.multiple_of(me_inner * rows, rows), rows), :], out_columns, out_recv
    )

    def second(index):
        target = (me_inner + 1 + index) % inner
        piece = pl.ds(pl.multiple_of(target * rows, rows), rows)
        result[piece, :] = lax.dot_general(
            h_panel[piece, :], r_panel[...], (((1,), (1,)), ((), ())),
            preferred_element_type=jnp.float32,
        ).astype(jnp.bfloat16)

        @pl.when(index < inner - 1)
        def _():
            out_copy(index).start()

    each(inner, second)
    out_own.start()

    each(data - 1, lambda index: sums_copy(index).wait_send())
    each(cores - 1, lambda index: mean_copy(index).wait_send())
    each(count - 1, lambda index: part_copy(index).wait_send())
    each(data - 1, lambda index: w_copy(index).wait_send())
    each(plane - 1, lambda index: l_copy(index).wait_send())
    each(outer - 1, lambda index: r_copy(index).wait_send())

    @pl.when(jnp.logical_not(keeps))
    def _():
        r_copy(outer - 1).wait_send()

    each(plane - 1, lambda index: h_copy(index).wait_send())
    each(inner - 1, lambda index: out_copy(index).wait_send())
    store_l.wait()
    store_r.wait()
    pltpu.make_async_copy(out_ref, out_ref, out_recv).wait()


def fused(data, cores, layer_inputs, out_grads, weight_grad, left_inv, right_inv):
    outer, inner = split(data)
    plane = inner * cores
    count = data * cores
    rows, cols = left_inv.shape
    width = cols // inner
    tokens = layer_inputs.shape[0] * data
    sums = jnp.stack(
        [
            jnp.sum(layer_inputs, axis=0, dtype=jnp.float32),
            jnp.sum(out_grads, axis=0, dtype=jnp.float32),
        ]
    )
    whole = pl.BlockSpec(memory_space=pl.ANY)
    dma = pltpu.SemaphoreType.DMA
    precond, new_left, new_right = pl.pallas_call(
        functools.partial(kernel, outer, inner, cores, tokens),
        out_shape=(
            jax.ShapeDtypeStruct((rows, cols), jnp.bfloat16),
            jax.ShapeDtypeStruct((rows, cols), jnp.float32),
            jax.ShapeDtypeStruct((rows, cols), jnp.float32),
        ),
        in_specs=[pl.BlockSpec(memory_space=pltpu.VMEM), whole, whole, whole],
        out_specs=(whole, whole, whole),
        scratch_shapes=[
            pltpu.VMEM((data, 2, cols), jnp.float32),
            pltpu.VMEM((cores, 2, cols), jnp.float32),
            pltpu.VMEM((count, 2, rows), jnp.float32),
            pltpu.VMEM((data, 2, rows), jnp.float32),
            pltpu.VMEM((cores, 2, cols), jnp.float32),
            pltpu.VMEM((2, rows, 128), jnp.float32),
            pltpu.VMEM((rows, cols), jnp.float32),
            pltpu.VMEM((rows, cols), jnp.float32),
            pltpu.VMEM((rows, cols), jnp.bfloat16),
            pltpu.VMEM((data * rows, width), jnp.bfloat16),
            pltpu.VMEM((inner * rows, cores * cols), jnp.bfloat16),
            pltpu.VMEM((width, cores * cols), jnp.bfloat16),
            pltpu.VMEM((inner * rows, cores * cols), jnp.bfloat16),
            pltpu.VMEM((inner * rows, width), jnp.bfloat16),
            dma((2,)),
            dma((2,)),
            dma((data,)),
            dma((cores,)),
            dma((count,)),
            dma((data,)),
            dma((plane,)),
            dma((outer,)),
            dma((plane,)),
            dma((inner,)),
        ]
        + [dma(())] * 8,
        compiler_params=pltpu.CompilerParams(
            collective_id=0, has_side_effects=True, vmem_limit_bytes=60 * 1024 * 1024
        ),
        cost_estimate=pl.CostEstimate(
            flops=4 * inner * rows * width * cores * cols,
            bytes_accessed=16 * rows * cols,
            transcendentals=0,
        ),
    )(sums, weight_grad, left_inv, jnp.transpose(right_inv))
    return precond, new_left, jnp.transpose(new_right)


def dispatch(data, cores, *arrays):
    outer, inner = split(data)
    rows, cols = arrays[3].shape
    fits = (
        cores > 1
        and inner > 1
        and outer % cores == 0
        and rows % 32 == 0
        and cols % (128 * inner) == 0
        and cols * cores == rows * data
    )
    if fits:
        return fused(data, cores, *arrays)
    return gathered(*arrays)


def solution(mesh):
    in_specs = (
        P("dp", "factor"),
        P("dp", "factor"),
        P("dp", "factor"),
        P("dp", "factor"),
        P("factor", "dp"),
    )
    out_specs = (P("dp", "factor"), P("dp", "factor"), P("factor", "dp"))
    return jax.shard_map(
        functools.partial(dispatch, mesh.shape["dp"], mesh.shape["factor"]), mesh=mesh, in_specs=in_specs, out_specs=out_specs, check_vma=False
    )
```

```python
import functools
import jax
import jax.numpy as jnp
from jax import lax
from jax.experimental import pallas as pl
from jax.experimental.pallas import tpu as pltpu
from jax.sharding import PartitionSpec as P

decay = 0.9


def coefficient(quadratic):
    return (1.0 - decay) / (decay * decay * (1.0 + (1.0 - decay) / decay * quadratic))


def gathered(layer_inputs, out_grads, weight_grad, left_inv, right_inv):
    highest = lax.Precision.HIGHEST
    token_count = layer_inputs.shape[0] * lax.axis_size("dp")
    act_local = jnp.sum(layer_inputs, axis=0, dtype=jnp.float32)
    grad_local = jnp.sum(out_grads, axis=0, dtype=jnp.float32)
    act_sums, grad_sums = lax.psum((act_local, grad_local), "dp")
    mean_act = act_sums / token_count
    mean_grad = grad_sums / token_count
    whole_act, whole_grad = (
        lax.all_gather(mean_act, "factor", axis=0, tiled=True),
        lax.all_gather(mean_grad, "factor", axis=0, tiled=True),
    )
    left_rows, left_cols = left_inv.shape
    right_rows, right_cols = right_inv.shape
    data_index = lax.axis_index("dp")
    act_rows = lax.dynamic_slice_in_dim(whole_act, data_index * left_rows, left_rows)
    grad_cols = lax.dynamic_slice_in_dim(whole_grad, data_index * right_cols, right_cols)
    row_terms = jnp.dot(left_inv, mean_act, precision=highest)
    col_terms = jnp.dot(mean_grad, right_inv, precision=highest)
    left_image_rows, right_image_cols = lax.psum((row_terms, col_terms), "factor")
    left_partial = jnp.dot(act_rows, left_inv, precision=highest)
    right_partial = jnp.dot(right_inv, grad_cols, precision=highest)
    left_image_cols, right_image_rows = lax.psum((left_partial, right_partial), "dp")
    left_quad, right_quad = lax.psum(
        (jnp.sum(mean_act * left_image_cols), jnp.sum(mean_grad * right_image_rows)), "factor"
    )
    left_coef = coefficient(left_quad)
    right_coef = coefficient(right_quad)
    new_left = left_inv / decay - left_coef * left_image_rows[:, None] * left_image_cols[None, :]
    new_right = (
        right_inv / decay - right_coef * right_image_rows[:, None] * right_image_cols[None, :]
    )
    left_half = new_left.astype(jnp.bfloat16)
    right_half = new_right.astype(jnp.bfloat16)
    left_wide = lax.all_gather(left_half, "factor", axis=1, tiled=True)
    matched = left_wide
    hidden_sum = jnp.dot(
        matched,
        lax.all_gather(weight_grad, "dp", axis=0, tiled=True),
        preferred_element_type=jnp.float32,
    )
    hidden = hidden_sum.astype(jnp.bfloat16)
    hidden_wide = lax.all_gather(hidden, "factor", axis=1, tiled=True)
    matched = hidden_wide
    precond = lax.dot_general(
        matched,
        lax.all_gather(right_half, "dp", axis=1, tiled=True),
        (((1,), (1,)), ((), ())),
        preferred_element_type=jnp.float32,
    )
    return (precond.astype(jnp.bfloat16), new_left, new_right)


MESH = pl.DeviceIdType.MESH


def split(count):
    inner = 1
    for size in range(1, count + 1):
        if count % size == 0 and size * size <= count:
            inner = size
    return count // inner, inner


def kernel(
    outer, inner, cores, tokens,
    sums_ref, w_ref, l_ref, r_ref,
    out_ref, new_l_ref, new_r_ref,
    sums_all, mean_all, part_all, image, image_half, columns,
    l_buf, r_buf, r_stage, w_panel, l_panel, r_panel, h_panel, result,
    load_sem, store_sem,
    sums_send, mean_send, part_send, w_send, l_send, h_send, out_send,
    wz_send, wz_recv, rz_send, rz_recv, lc_send, hc_send, rc_send,
    sums_recv, mean_recv, part_recv, w_recv, l_recv, h_recv, out_recv, lc_recv, hc_recv, rc_recv,
):
    data = outer * inner
    count = data * cores
    slots = outer // cores
    rows, cols = l_buf.shape
    width = w_panel.shape[1]
    me_data = lax.axis_index("dp")
    me_core = lax.axis_index("factor")
    me = me_data * cores + me_core
    me_outer = me_data // inner
    me_inner = me_data % inner

    def remote(src, dst, send, recv, target_data, target_core):
        return pltpu.make_async_remote_copy(
            src_ref=src, dst_ref=dst, send_sem=send, recv_sem=recv,
            device_id=(target_data, target_core), device_id_type=MESH,
        )

    def each(total, body):
        def step(index, carry):
            body(index)
            return carry

        lax.fori_loop(0, total, step, 0)

    load_l = pltpu.make_async_copy(l_ref, l_buf, load_sem.at[0])
    load_r = pltpu.make_async_copy(r_ref, r_buf, load_sem.at[1])
    load_l.start()
    load_r.start()
    sums_all[me_data] = sums_ref[...]

    barrier = pltpu.get_barrier_semaphore()

    def greet(index):
        target = (me + 1 + index) % count
        pl.semaphore_signal(
            barrier, inc=1, device_id=(target // cores, target % cores), device_id_type=MESH
        )

    each(count - 1, greet)
    pl.semaphore_wait(barrier, count - 1)

    def sums_copy(index):
        target = (me_data + 1 + index) % data
        return remote(
            sums_all.at[me_data], sums_all.at[me_data],
            sums_send.at[index], sums_recv, target, me_core,
        )

    each(data - 1, lambda index: sums_copy(index).start())

    strip = inner * rows

    def peer(index):
        return me_outer * inner + (me_inner + 1 + index) % inner, me_core

    def w_piece(block):
        return w_ref.at[:, pl.ds(pl.multiple_of(block * width, width), width)]

    w_place = w_panel.at[pl.ds(pl.multiple_of(me_data * rows, rows), rows), :]

    def w_copy(index):
        target = (me_inner + 1 + index) % inner
        return remote(w_piece(target), w_place, w_send.at[index], w_recv, *peer(index))

    def chain(step, block_of, send, recv, act):
        right, left = me_outer - step, me_outer + step

        @pl.when(jnp.logical_and(right >= 0, me_outer < outer - 1))
        def _():
            act(remote(
                block_of(right), block_of(right), send.at[0, step], recv.at[right],
                me_data + inner, me_core,
            ))

        @pl.when(jnp.logical_and(left < outer, me_outer > 0))
        def _():
            act(remote(
                block_of(left), block_of(left), send.at[1, step], recv.at[left],
                me_data - inner, me_core,
            ))

    def arrived(step, block_of, recv, after=None):
        for block in (me_outer - 1 - step, me_outer + 1 + step):

            @pl.when(jnp.logical_and(block >= 0, block < outer))
            def _(block=block):
                pltpu.make_async_copy(block_of(block), block_of(block), recv.at[block]).wait()
                if after is not None:
                    after(block)

    def start(copy):
        copy.start()

    def w_block(block):
        return w_panel.at[pl.ds(pl.multiple_of(block * strip, strip), strip), :]

    def r_block(block):
        return r_stage.at[block]

    each(inner - 1, lambda index: w_copy(index).start())
    pltpu.make_async_copy(w_piece(me_inner), w_place, w_recv).start()

    some = sums_all.at[pl.ds(0, data - 1)]
    pltpu.make_async_copy(some, some, sums_recv).wait()
    mean = jnp.sum(sums_all[...], axis=0) / tokens
    mean_all[me_core] = mean

    def mean_copy(index):
        target = (me_core + 1 + index) % cores
        return remote(
            mean_all.at[me_core], mean_all.at[me_core],
            mean_send.at[index], mean_recv, me_data, target,
        )

    each(cores - 1, lambda index: mean_copy(index).start())
    load_l.wait()
    load_r.wait()
    step = 32
    for side, buf in enumerate((l_buf, r_buf)):

        def partial(index, side=side, buf=buf):
            piece = pl.ds(pl.multiple_of(index * step, step), step)
            total = jnp.sum(
                buf[piece, :] * mean_all[me_core][side : side + 1, :], axis=1, keepdims=True
            )
            columns[side, piece, :] = jnp.broadcast_to(total, (step, 128))

        each(rows // step, partial)
    part_all[me] = jnp.concatenate(
        [jnp.transpose(columns[side])[0:1, :] for side in range(2)], axis=0
    )

    def part_copy(index):
        target = (me + 1 + index) % count
        return remote(
            part_all.at[me], part_all.at[me],
            part_send.at[index], part_recv, target // cores, target % cores,
        )

    each(count - 1, lambda index: part_copy(index).start())

    other_means = mean_all.at[pl.ds(0, cores - 1)]
    pltpu.make_async_copy(other_means, other_means, mean_recv).wait()
    other_parts = part_all.at[pl.ds(0, count - 1)]
    pltpu.make_async_copy(other_parts, other_parts, part_recv).wait()
    pltpu.make_async_copy(w_block(me_outer), w_block(me_outer), w_recv).wait()
    chain(0, w_block, wz_send, wz_recv, start)

    per_core = data // cores
    quad = jnp.zeros((2, 1), jnp.float32)
    for core in range(cores):
        blocks = []
        for block in range(core * per_core, (core + 1) * per_core):
            total = part_all[block * cores]
            for other in range(1, cores):
                total = total + part_all[block * cores + other]
            image[block] = total
            blocks.append(total)
        half = jnp.concatenate(blocks, axis=1)
        image_half[core] = half
        quad = quad + jnp.sum(mean_all[core] * half, axis=1, keepdims=True)
    coef = (1.0 - decay) / (decay * decay * (1.0 + (1.0 - decay) / decay * quad))
    scaled = image[me_data] * coef
    for side in range(2):
        columns[side] = jnp.transpose(jnp.broadcast_to(scaled[side : side + 1, :], (128, rows)))

    core_columns = pl.ds(pl.multiple_of(me_core * cols, cols), cols)
    l_own = l_panel.at[pl.ds(pl.multiple_of(me_inner * rows, rows), rows), core_columns]

    def l_copy(index):
        return remote(l_own, l_own, l_send.at[index], l_recv, *peer(index))

    for side, buf in enumerate((l_buf, r_buf)):

        def update(index, side=side, buf=buf):
            piece = pl.ds(pl.multiple_of(index * step, step), step)
            fresh = buf[piece, :] * (1.0 / decay) - (
                columns[side, piece, :][:, 0:1] * image_half[me_core][side : side + 1, :]
            )
            buf[piece, :] = fresh
            if side == 0:
                l_panel[
                    pl.ds(pl.multiple_of(me_inner * rows + index * step, step), step),
                    pl.ds(pl.multiple_of(me_core * cols, cols), cols),
                ] = fresh.astype(jnp.bfloat16)
            else:
                r_stage[me_outer, piece, :] = fresh.astype(jnp.bfloat16)

        each(rows // step, update)
        if side == 0:
            each(inner - 1, lambda index: l_copy(index).start())

    store_l = pltpu.make_async_copy(l_buf, new_l_ref, store_sem.at[0])
    store_r = pltpu.make_async_copy(r_buf, new_r_ref, store_sem.at[1])
    store_l.start()
    store_r.start()

    def core_copy(panel, send, recv, index):
        slab = panel.at[:, core_columns]
        return remote(slab, slab, send.at[index], recv, me_data, (me_core + 1 + index) % cores)

    def whole_rows(panel, recv, send, recv_core, part):
        pltpu.make_async_copy(part, part, recv).wait()
        each(cores - 1, lambda index: core_copy(panel, send, recv_core, index).start())

    def core_wait(panel, recv):
        others = panel.at[:, pl.ds(0, (cores - 1) * cols)]
        pltpu.make_async_copy(others, others, recv).wait()

    def r_place(block):
        return r_panel.at[
            pl.ds(pl.multiple_of((block % slots) * rows, rows), rows), core_columns
        ]

    def r_relay(block):
        return remote(
            r_block(block), r_place(block), rc_send.at[block], rc_recv, me_data, block // slots
        )

    def r_spread(block):
        @pl.when(block // slots == me_core)
        def _():
            pltpu.make_async_copy(r_block(block), r_place(block), rc_recv).start()

        @pl.when(block // slots != me_core)
        def _():
            r_relay(block).start()

    for step_z in range(1, outer - 1):
        arrived(step_z - 1, w_block, wz_recv)
        chain(step_z, w_block, wz_send, wz_recv, start)
    whole_rows(
        l_panel, l_recv, lc_send, lc_recv, l_panel.at[pl.ds(0, (inner - 1) * rows), core_columns]
    )
    arrived(outer - 2, w_block, wz_recv)
    chain(0, r_block, rz_send, rz_recv, start)
    r_spread(me_outer)
    core_wait(l_panel, lc_recv)

    h_columns = pl.ds(pl.multiple_of(me_core * cols + me_inner * width, width), width)

    def first(index):
        piece = pl.ds(pl.multiple_of(index * rows, rows), rows)
        h_panel[piece, h_columns] = jnp.dot(
            l_panel[piece, :], w_panel[...], preferred_element_type=jnp.float32
        ).astype(jnp.bfloat16)

    each(inner, first)

    h_own = h_panel.at[:, h_columns]

    def h_copy(index):
        return remote(h_own, h_own, h_send.at[index], h_recv, *peer(index))

    each(inner - 1, lambda index: h_copy(index).start())

    for step_z in range(1, outer - 1):
        arrived(step_z - 1, r_block, rz_recv, r_spread)
        chain(step_z, r_block, rz_send, rz_recv, start)
    whole_rows(
        h_panel, h_recv, hc_send, hc_recv, h_panel.at[:, pl.ds(0, (inner - 1) * width)]
    )
    arrived(outer - 2, r_block, rz_recv, r_spread)
    pltpu.make_async_copy(r_panel, r_panel, rc_recv).wait()
    core_wait(h_panel, hc_recv)

    out_place = out_ref.at[me_inner]

    def out_copy(index):
        target = (me_inner + 1 + index) % inner
        return remote(
            result.at[pl.ds(pl.multiple_of(target * rows, rows), rows), :], out_place,
            out_send.at[index], out_recv, me_outer * inner + target, me_core,
        )

    out_own = pltpu.make_async_copy(
        result.at[pl.ds(pl.multiple_of(me_inner * rows, rows), rows), :], out_place, out_recv
    )

    def second(index):
        target = (me_inner + 1 + index) % inner
        piece = pl.ds(pl.multiple_of(target * rows, rows), rows)
        result[piece, :] = lax.dot_general(
            h_panel[piece, :], r_panel[...], (((1,), (1,)), ((), ())),
            preferred_element_type=jnp.float32,
        ).astype(jnp.bfloat16)

        @pl.when(index < inner - 1)
        def _():
            out_copy(index).start()

    each(inner, second)
    out_own.start()

    each(data - 1, lambda index: sums_copy(index).wait_send())
    each(cores - 1, lambda index: mean_copy(index).wait_send())
    each(count - 1, lambda index: part_copy(index).wait_send())
    each(inner - 1, lambda index: w_copy(index).wait_send())
    each(inner - 1, lambda index: l_copy(index).wait_send())
    each(inner - 1, lambda index: h_copy(index).wait_send())
    each(inner - 1, lambda index: out_copy(index).wait_send())
    each(cores - 1, lambda index: core_copy(l_panel, lc_send, lc_recv, index).wait_send())
    each(cores - 1, lambda index: core_copy(h_panel, hc_send, hc_recv, index).wait_send())
    for step_z in range(outer - 1):
        chain(step_z, w_block, wz_send, wz_recv, lambda copy: copy.wait_send())
        chain(step_z, r_block, rz_send, rz_recv, lambda copy: copy.wait_send())
    for block in range(outer):

        @pl.when(block // slots != me_core)
        def _(block=block):
            r_relay(block).wait_send()

    store_l.wait()
    store_r.wait()
    pltpu.make_async_copy(out_ref, out_ref, out_recv).wait()


def fused(data, cores, layer_inputs, out_grads, weight_grad, left_inv, right_inv):
    outer, inner = split(data)
    count = data * cores
    rows, cols = left_inv.shape
    width = cols // inner
    tokens = layer_inputs.shape[0] * data
    sums = jnp.stack(
        [
            jnp.sum(layer_inputs, axis=0, dtype=jnp.float32),
            jnp.sum(out_grads, axis=0, dtype=jnp.float32),
        ]
    )
    whole = pl.BlockSpec(memory_space=pl.ANY)
    dma = pltpu.SemaphoreType.DMA
    precond, new_left, new_right = pl.pallas_call(
        functools.partial(kernel, outer, inner, cores, tokens),
        out_shape=(
            jax.ShapeDtypeStruct((inner, rows, width), jnp.bfloat16),
            jax.ShapeDtypeStruct((rows, cols), jnp.float32),
            jax.ShapeDtypeStruct((rows, cols), jnp.float32),
        ),
        in_specs=[pl.BlockSpec(memory_space=pltpu.VMEM), whole, whole, whole],
        out_specs=(whole, whole, whole),
        scratch_shapes=[
            pltpu.VMEM((data, 2, cols), jnp.float32),
            pltpu.VMEM((cores, 2, cols), jnp.float32),
            pltpu.VMEM((count, 2, rows), jnp.float32),
            pltpu.VMEM((data, 2, rows), jnp.float32),
            pltpu.VMEM((cores, 2, cols), jnp.float32),
            pltpu.VMEM((2, rows, 128), jnp.float32),
            pltpu.VMEM((rows, cols), jnp.float32),
            pltpu.VMEM((rows, cols), jnp.float32),
            pltpu.VMEM((outer, rows, cols), jnp.bfloat16),
            pltpu.VMEM((data * rows, width), jnp.bfloat16),
            pltpu.VMEM((inner * rows, cores * cols), jnp.bfloat16),
            pltpu.VMEM((width, cores * cols), jnp.bfloat16),
            pltpu.VMEM((inner * rows, cores * cols), jnp.bfloat16),
            pltpu.VMEM((inner * rows, width), jnp.bfloat16),
            dma((2,)),
            dma((2,)),
            dma((data,)),
            dma((cores,)),
            dma((count,)),
            dma((inner,)),
            dma((inner,)),
            dma((inner,)),
            dma((inner,)),
            dma((2, outer)),
            dma((outer,)),
            dma((2, outer)),
            dma((outer,)),
            dma((cores,)),
            dma((cores,)),
            dma((outer,)),
        ]
        + [dma(())] * 10,
        compiler_params=pltpu.CompilerParams(
            collective_id=0, has_side_effects=True, vmem_limit_bytes=60 * 1024 * 1024
        ),
        cost_estimate=pl.CostEstimate(
            flops=4 * inner * rows * width * cores * cols,
            bytes_accessed=16 * rows * cols,
            transcendentals=0,
        ),
    )(sums, weight_grad, left_inv, jnp.transpose(right_inv))
    precond = precond.reshape(inner, rows, width // rows, rows)
    precond = jnp.transpose(precond, (1, 2, 0, 3)).reshape(rows, cols)
    return precond, new_left, jnp.transpose(new_right)


def dispatch(data, cores, *arrays):
    outer, inner = split(data)
    rows, cols = arrays[3].shape
    fits = (
        cores > 1
        and inner > 1
        and outer % cores == 0
        and rows % 32 == 0
        and cols % (128 * inner) == 0
        and cols * cores == rows * data
    )
    if fits:
        return fused(data, cores, *arrays)
    return gathered(*arrays)


def solution(mesh):
    in_specs = (
        P("dp", "factor"),
        P("dp", "factor"),
        P("dp", "factor"),
        P("dp", "factor"),
        P("factor", "dp"),
    )
    out_specs = (P("dp", "factor"), P("dp", "factor"), P("factor", "dp"))
    return jax.shard_map(
        functools.partial(dispatch, mesh.shape["dp"], mesh.shape["factor"]), mesh=mesh, in_specs=in_specs, out_specs=out_specs, check_vma=False
    )
```

```python
import functools
import jax
import jax.numpy as jnp
from jax import lax
from jax.experimental import pallas as pl
from jax.experimental.pallas import tpu as pltpu
from jax.sharding import PartitionSpec as P

decay = 0.9


def coefficient(quadratic):
    return (1.0 - decay) / (decay * decay * (1.0 + (1.0 - decay) / decay * quadratic))


def gathered(layer_inputs, out_grads, weight_grad, left_inv, right_inv):
    highest = lax.Precision.HIGHEST
    token_count = layer_inputs.shape[0] * lax.axis_size("dp")
    act_local = jnp.sum(layer_inputs, axis=0, dtype=jnp.float32)
    grad_local = jnp.sum(out_grads, axis=0, dtype=jnp.float32)
    act_sums, grad_sums = lax.psum((act_local, grad_local), "dp")
    mean_act = act_sums / token_count
    mean_grad = grad_sums / token_count
    whole_act, whole_grad = (
        lax.all_gather(mean_act, "factor", axis=0, tiled=True),
        lax.all_gather(mean_grad, "factor", axis=0, tiled=True),
    )
    left_rows, left_cols = left_inv.shape
    right_rows, right_cols = right_inv.shape
    data_index = lax.axis_index("dp")
    act_rows = lax.dynamic_slice_in_dim(whole_act, data_index * left_rows, left_rows)
    grad_cols = lax.dynamic_slice_in_dim(whole_grad, data_index * right_cols, right_cols)
    row_terms = jnp.dot(left_inv, mean_act, precision=highest)
    col_terms = jnp.dot(mean_grad, right_inv, precision=highest)
    left_image_rows, right_image_cols = lax.psum((row_terms, col_terms), "factor")
    left_partial = jnp.dot(act_rows, left_inv, precision=highest)
    right_partial = jnp.dot(right_inv, grad_cols, precision=highest)
    left_image_cols, right_image_rows = lax.psum((left_partial, right_partial), "dp")
    left_quad, right_quad = lax.psum(
        (jnp.sum(mean_act * left_image_cols), jnp.sum(mean_grad * right_image_rows)), "factor"
    )
    left_coef = coefficient(left_quad)
    right_coef = coefficient(right_quad)
    new_left = left_inv / decay - left_coef * left_image_rows[:, None] * left_image_cols[None, :]
    new_right = (
        right_inv / decay - right_coef * right_image_rows[:, None] * right_image_cols[None, :]
    )
    left_half = new_left.astype(jnp.bfloat16)
    right_half = new_right.astype(jnp.bfloat16)
    left_wide = lax.all_gather(left_half, "factor", axis=1, tiled=True)
    matched = left_wide
    hidden_sum = jnp.dot(
        matched,
        lax.all_gather(weight_grad, "dp", axis=0, tiled=True),
        preferred_element_type=jnp.float32,
    )
    hidden = hidden_sum.astype(jnp.bfloat16)
    hidden_wide = lax.all_gather(hidden, "factor", axis=1, tiled=True)
    matched = hidden_wide
    precond = lax.dot_general(
        matched,
        lax.all_gather(right_half, "dp", axis=1, tiled=True),
        (((1,), (1,)), ((), ())),
        preferred_element_type=jnp.float32,
    )
    return (precond.astype(jnp.bfloat16), new_left, new_right)


MESH = pl.DeviceIdType.MESH


def split(count):
    inner = 1
    for size in range(1, count + 1):
        if count % size == 0 and size * size <= count:
            inner = size
    return count // inner, inner


def kernel(
    outer, inner, cores, tokens,
    x_ref, g_ref, w_ref, l_ref, r_ref,
    out_ref, new_l_ref, new_r_ref,
    sums_all, mean_all, part_all, image, image_half, columns,
    l_buf, r_buf, r_stage, w_panel, l_panel, r_panel, h_panel, result, pieces,
    load_sem, store_sem,
    sums_send, mean_send, part_send, w_send, l_send, h_send, out_send,
    wz_send, wz_recv, rz_send, rz_recv, lc_send, hc_send, rc_send,
    sums_recv, mean_recv, part_recv, w_recv, l_recv, h_recv, out_recv, lc_recv, hc_recv, rc_recv,
):
    data = outer * inner
    count = data * cores
    slots = outer // cores
    rows, cols = l_buf.shape
    width = w_panel.shape[1]
    me_data = lax.axis_index("dp")
    me_core = lax.axis_index("factor")
    me = me_data * cores + me_core
    me_outer = me_data // inner
    me_inner = me_data % inner

    def remote(src, dst, send, recv, target_data, target_core):
        return pltpu.make_async_remote_copy(
            src_ref=src, dst_ref=dst, send_sem=send, recv_sem=recv,
            device_id=(target_data, target_core), device_id_type=MESH,
        )

    def each(total, body):
        def step(index, carry):
            body(index)
            return carry

        lax.fori_loop(0, total, step, 0)

    token_rows = x_ref.shape[0]
    tokens_in = [
        pltpu.make_async_copy(
            ref, h_panel.at[pl.ds(0, token_rows), pl.ds(side * cols, cols)], load_sem.at[2 + side]
        )
        for side, ref in enumerate((x_ref, g_ref))
    ]
    for load in tokens_in:
        load.start()
    load_l = pltpu.make_async_copy(l_ref, l_buf, load_sem.at[0])
    load_r = pltpu.make_async_copy(r_ref, r_buf, load_sem.at[1])
    load_l.start()
    load_r.start()

    barrier = pltpu.get_barrier_semaphore()

    def greet(index):
        target = (me + 1 + index) % count
        pl.semaphore_signal(
            barrier, inc=1, device_id=(target // cores, target % cores), device_id_type=MESH
        )

    each(count - 1, greet)
    pl.semaphore_wait(barrier, count - 1)

    def sums_copy(index):
        target = (me_data + 1 + index) % data
        return remote(
            sums_all.at[me_data], sums_all.at[me_data],
            sums_send.at[index], sums_recv, target, me_core,
        )

    strip = inner * rows

    def peer(index):
        return me_outer * inner + (me_inner + 1 + index) % inner, me_core

    def w_piece(block):
        return w_ref.at[:, pl.ds(pl.multiple_of(block * width, width), width)]

    w_place = w_panel.at[pl.ds(pl.multiple_of(me_data * rows, rows), rows), :]

    def w_copy(index):
        target = (me_inner + 1 + index) % inner
        return remote(w_piece(target), w_place, w_send.at[index], w_recv, *peer(index))

    def chain(step, block_of, send, recv, act):
        right, left = me_outer - step, me_outer + step

        @pl.when(jnp.logical_and(right >= 0, me_outer < outer - 1))
        def _():
            act(remote(
                block_of(right), block_of(right), send.at[0, step], recv.at[right],
                me_data + inner, me_core,
            ))

        @pl.when(jnp.logical_and(left < outer, me_outer > 0))
        def _():
            act(remote(
                block_of(left), block_of(left), send.at[1, step], recv.at[left],
                me_data - inner, me_core,
            ))

    def arrived(step, block_of, recv, after=None):
        for block in (me_outer - 1 - step, me_outer + 1 + step):

            @pl.when(jnp.logical_and(block >= 0, block < outer))
            def _(block=block):
                pltpu.make_async_copy(block_of(block), block_of(block), recv.at[block]).wait()
                if after is not None:
                    after(block)

    def start(copy):
        copy.start()

    def w_block(block):
        return w_panel.at[pl.ds(pl.multiple_of(block * strip, strip), strip), :]

    def r_block(block):
        return r_stage.at[block]

    each(inner - 1, lambda index: w_copy(index).start())
    pltpu.make_async_copy(w_piece(me_inner), w_place, w_recv).start()

    for side in range(2):
        tokens_in[side].wait()
        for block in range(inner):
            first_column = side * cols + block * width

            def add(index, total, first_column=first_column):
                piece = h_panel[
                    pl.ds(pl.multiple_of(index * 64, 64), 64), pl.ds(first_column, width)
                ].astype(jnp.float32)
                return total + jnp.sum(piece.reshape(8, 8, width), axis=0)

            total = lax.fori_loop(
                0, token_rows // 64, add, jnp.zeros((8, width), jnp.float32)
            )
            sums_all[me_data, side : side + 1, pl.ds(block * width, width)] = jnp.sum(
                total, axis=0, keepdims=True
            )

    each(data - 1, lambda index: sums_copy(index).start())

    some = sums_all.at[pl.ds(0, data - 1)]
    pltpu.make_async_copy(some, some, sums_recv).wait()
    mean = jnp.sum(sums_all[...], axis=0) / tokens
    mean_all[me_core] = mean

    def mean_copy(index):
        target = (me_core + 1 + index) % cores
        return remote(
            mean_all.at[me_core], mean_all.at[me_core],
            mean_send.at[index], mean_recv, me_data, target,
        )

    each(cores - 1, lambda index: mean_copy(index).start())
    load_l.wait()
    load_r.wait()
    step = 32
    for side, buf in enumerate((l_buf, r_buf)):

        def partial(index, side=side, buf=buf):
            piece = pl.ds(pl.multiple_of(index * step, step), step)
            total = jnp.sum(
                buf[piece, :] * mean_all[me_core][side : side + 1, :], axis=1, keepdims=True
            )
            columns[side, piece, :] = jnp.broadcast_to(total, (step, 128))

        each(rows // step, partial)
    part_all[me] = jnp.concatenate(
        [jnp.transpose(columns[side])[0:1, :] for side in range(2)], axis=0
    )

    def part_copy(index):
        target = (me + 1 + index) % count
        return remote(
            part_all.at[me], part_all.at[me],
            part_send.at[index], part_recv, target // cores, target % cores,
        )

    each(count - 1, lambda index: part_copy(index).start())

    pltpu.make_async_copy(w_block(me_outer), w_block(me_outer), w_recv).wait()
    chain(0, w_block, wz_send, wz_recv, start)

    other_means = mean_all.at[pl.ds(0, cores - 1)]
    pltpu.make_async_copy(other_means, other_means, mean_recv).wait()
    other_parts = part_all.at[pl.ds(0, count - 1)]
    pltpu.make_async_copy(other_parts, other_parts, part_recv).wait()

    per_core = data // cores
    quad = jnp.zeros((2, 1), jnp.float32)
    for core in range(cores):
        blocks = []
        for block in range(core * per_core, (core + 1) * per_core):
            total = part_all[block * cores]
            for other in range(1, cores):
                total = total + part_all[block * cores + other]
            image[block] = total
            blocks.append(total)
        half = jnp.concatenate(blocks, axis=1)
        image_half[core] = half
        quad = quad + jnp.sum(mean_all[core] * half, axis=1, keepdims=True)
    coef = (1.0 - decay) / (decay * decay * (1.0 + (1.0 - decay) / decay * quad))
    scaled = image[me_data] * coef
    for side in range(2):
        columns[side] = jnp.transpose(jnp.broadcast_to(scaled[side : side + 1, :], (128, rows)))

    core_columns = pl.ds(pl.multiple_of(me_core * cols, cols), cols)
    l_own = l_panel.at[pl.ds(pl.multiple_of(me_inner * rows, rows), rows), core_columns]

    def l_copy(index):
        return remote(l_own, l_own, l_send.at[index], l_recv, *peer(index))

    for side, buf in enumerate((l_buf, r_buf)):

        def update(index, side=side, buf=buf):
            piece = pl.ds(pl.multiple_of(index * step, step), step)
            fresh = buf[piece, :] * (1.0 / decay) - (
                columns[side, piece, :][:, 0:1] * image_half[me_core][side : side + 1, :]
            )
            buf[piece, :] = fresh
            if side == 0:
                l_panel[
                    pl.ds(pl.multiple_of(me_inner * rows + index * step, step), step),
                    pl.ds(pl.multiple_of(me_core * cols, cols), cols),
                ] = fresh.astype(jnp.bfloat16)
            else:
                r_stage[me_outer, piece, :] = fresh.astype(jnp.bfloat16)

        each(rows // step, update)
        if side == 0:
            each(inner - 1, lambda index: l_copy(index).start())

    store_l = pltpu.make_async_copy(l_buf, new_l_ref, store_sem.at[0])
    store_r = pltpu.make_async_copy(r_buf, new_r_ref, store_sem.at[1])
    store_l.start()
    store_r.start()

    def core_copy(panel, send, recv, index):
        slab = panel.at[:, core_columns]
        return remote(slab, slab, send.at[index], recv, me_data, (me_core + 1 + index) % cores)

    def whole_rows(panel, recv, send, recv_core, part):
        pltpu.make_async_copy(part, part, recv).wait()
        each(cores - 1, lambda index: core_copy(panel, send, recv_core, index).start())

    def core_wait(panel, recv):
        others = panel.at[:, pl.ds(0, (cores - 1) * cols)]
        pltpu.make_async_copy(others, others, recv).wait()

    def r_place(block):
        return r_panel.at[
            pl.ds(pl.multiple_of((block % slots) * rows, rows), rows), core_columns
        ]

    def r_relay(block):
        return remote(
            r_block(block), r_place(block), rc_send.at[block], rc_recv, me_data, block // slots
        )

    def r_spread(block):
        @pl.when(block // slots == me_core)
        def _():
            pltpu.make_async_copy(r_block(block), r_place(block), rc_recv).start()

        @pl.when(block // slots != me_core)
        def _():
            r_relay(block).start()

    for step_z in range(1, outer - 1):
        arrived(step_z - 1, w_block, wz_recv)
        chain(step_z, w_block, wz_send, wz_recv, start)
    whole_rows(
        l_panel, l_recv, lc_send, lc_recv, l_panel.at[pl.ds(0, (inner - 1) * rows), core_columns]
    )
    arrived(outer - 2, w_block, wz_recv)
    chain(0, r_block, rz_send, rz_recv, start)
    r_spread(me_outer)
    core_wait(l_panel, lc_recv)

    h_columns = pl.ds(pl.multiple_of(me_core * cols + me_inner * width, width), width)

    def tile(index):
        return pl.ds(pl.multiple_of(index * rows, rows), rows)

    def h_copy(index, other):
        own = h_panel.at[tile(index), h_columns]
        return remote(own, own, h_send.at[index, other], h_recv.at[index], *peer(other))

    def h_core(index, other):
        slab = h_panel.at[tile(index), core_columns]
        return remote(
            slab, slab, hc_send.at[index, other], hc_recv.at[index],
            me_data, (me_core + 1 + other) % cores,
        )

    def first(index):
        piece = tile(index)
        h_panel[piece, h_columns] = jnp.dot(
            l_panel[piece, :], w_panel[...], preferred_element_type=jnp.float32
        ).astype(jnp.bfloat16)
        for other in range(inner - 1):
            h_copy(index, other).start()

    def pass_on(index):
        peers = h_panel.at[tile(index), pl.ds(0, (inner - 1) * width)]
        pltpu.make_async_copy(peers, peers, h_recv.at[index]).wait()
        for other in range(cores - 1):
            h_core(index, other).start()

    def h_done(index):
        for other in range(inner - 1):
            h_copy(index, other).wait_send()
        for other in range(cores - 1):
            h_core(index, other).wait_send()

    each(inner, first)

    for step_z in range(1, outer - 1):
        arrived(step_z - 1, r_block, rz_recv, r_spread)
        chain(step_z, r_block, rz_send, rz_recv, start)
    each(inner, pass_on)
    arrived(outer - 2, r_block, rz_recv, r_spread)
    pltpu.make_async_copy(r_panel, r_panel, rc_recv).wait()

    out_place = pieces.at[me_inner]

    def out_copy(index):
        target = (me_inner + 1 + index) % inner
        return remote(
            result.at[pl.ds(pl.multiple_of(target * rows, rows), rows), :], out_place,
            out_send.at[index], out_recv, me_outer * inner + target, me_core,
        )

    out_own = pltpu.make_async_copy(
        result.at[pl.ds(pl.multiple_of(me_inner * rows, rows), rows), :], out_place, out_recv
    )

    def second(index):
        target = (me_inner + 1 + index) % inner
        piece = tile(target)
        others = h_panel.at[piece, pl.ds(0, (cores - 1) * cols)]
        pltpu.make_async_copy(others, others, hc_recv.at[target]).wait()
        result[piece, :] = lax.dot_general(
            h_panel[piece, :], r_panel[...], (((1,), (1,)), ((), ())),
            preferred_element_type=jnp.float32,
        ).astype(jnp.bfloat16)

        @pl.when(index < inner - 1)
        def _():
            out_copy(index).start()

    each(inner, second)
    out_own.start()

    each(data - 1, lambda index: sums_copy(index).wait_send())
    each(cores - 1, lambda index: mean_copy(index).wait_send())
    each(count - 1, lambda index: part_copy(index).wait_send())
    each(inner - 1, lambda index: w_copy(index).wait_send())
    each(inner - 1, lambda index: l_copy(index).wait_send())
    each(inner, h_done)
    each(inner - 1, lambda index: out_copy(index).wait_send())
    each(cores - 1, lambda index: core_copy(l_panel, lc_send, lc_recv, index).wait_send())
    for step_z in range(outer - 1):
        chain(step_z, w_block, wz_send, wz_recv, lambda copy: copy.wait_send())
        chain(step_z, r_block, rz_send, rz_recv, lambda copy: copy.wait_send())
    for block in range(outer):

        @pl.when(block // slots != me_core)
        def _(block=block):
            r_relay(block).wait_send()

    store_l.wait()
    store_r.wait()
    pltpu.make_async_copy(pieces, pieces, out_recv).wait()

    def assemble(index):
        piece = pl.ds(pl.multiple_of(index * step, step), step)
        parts = [pieces[block, piece, :] for block in range(inner)]
        r_stage[0, piece, :] = jnp.concatenate(
            [part[:, slot * rows : (slot + 1) * rows] for slot in range(slots) for part in parts],
            axis=1,
        )

    each(rows // step, assemble)
    store_out = pltpu.make_async_copy(r_stage.at[0], out_ref, store_sem.at[2])
    store_out.start()
    store_out.wait()


def fused(data, cores, layer_inputs, out_grads, weight_grad, left_inv, right_inv):
    outer, inner = split(data)
    count = data * cores
    rows, cols = left_inv.shape
    width = cols // inner
    tokens = layer_inputs.shape[0] * data
    whole = pl.BlockSpec(memory_space=pl.ANY)
    dma = pltpu.SemaphoreType.DMA
    precond, new_left, new_right = pl.pallas_call(
        functools.partial(kernel, outer, inner, cores, tokens),
        out_shape=(
            jax.ShapeDtypeStruct((rows, cols), jnp.bfloat16),
            jax.ShapeDtypeStruct((rows, cols), jnp.float32),
            jax.ShapeDtypeStruct((rows, cols), jnp.float32),
        ),
        in_specs=[whole] * 5,
        out_specs=(whole, whole, whole),
        scratch_shapes=[
            pltpu.VMEM((data, 2, cols), jnp.float32),
            pltpu.VMEM((cores, 2, cols), jnp.float32),
            pltpu.VMEM((count, 2, rows), jnp.float32),
            pltpu.VMEM((data, 2, rows), jnp.float32),
            pltpu.VMEM((cores, 2, cols), jnp.float32),
            pltpu.VMEM((2, rows, 128), jnp.float32),
            pltpu.VMEM((rows, cols), jnp.float32),
            pltpu.VMEM((rows, cols), jnp.float32),
            pltpu.VMEM((outer, rows, cols), jnp.bfloat16),
            pltpu.VMEM((data * rows, width), jnp.bfloat16),
            pltpu.VMEM((inner * rows, cores * cols), jnp.bfloat16),
            pltpu.VMEM((width, cores * cols), jnp.bfloat16),
            pltpu.VMEM((inner * rows, cores * cols), jnp.bfloat16),
            pltpu.VMEM((inner * rows, width), jnp.bfloat16),
            pltpu.VMEM((inner, rows, width), jnp.bfloat16),
            dma((4,)),
            dma((3,)),
            dma((data,)),
            dma((cores,)),
            dma((count,)),
            dma((inner,)),
            dma((inner,)),
            dma((inner, inner)),
            dma((inner,)),
            dma((2, outer)),
            dma((outer,)),
            dma((2, outer)),
            dma((outer,)),
            dma((cores,)),
            dma((inner, cores)),
            dma((outer,)),
            dma(()),
            dma(()),
            dma(()),
            dma(()),
            dma(()),
            dma((inner,)),
            dma(()),
            dma(()),
            dma((inner,)),
            dma(()),
        ],
        compiler_params=pltpu.CompilerParams(
            collective_id=0, has_side_effects=True, vmem_limit_bytes=62 * 1024 * 1024
        ),
        cost_estimate=pl.CostEstimate(
            flops=4 * inner * rows * width * cores * cols,
            bytes_accessed=16 * rows * cols,
            transcendentals=0,
        ),
    )(layer_inputs, out_grads, weight_grad, left_inv, jnp.transpose(right_inv))
    return precond, new_left, jnp.transpose(new_right)


def dispatch(data, cores, *arrays):
    outer, inner = split(data)
    rows, cols = arrays[3].shape
    fits = (
        cores > 1
        and inner > 1
        and outer % cores == 0
        and rows % 32 == 0
        and arrays[0].shape[0] % 64 == 0
        and arrays[0].shape[0] <= inner * rows
        and cols % (128 * inner) == 0
        and cols * cores == rows * data
    )
    if fits:
        return fused(data, cores, *arrays)
    return gathered(*arrays)


def solution(mesh):
    in_specs = (
        P("dp", "factor"),
        P("dp", "factor"),
        P("dp", "factor"),
        P("dp", "factor"),
        P("factor", "dp"),
    )
    out_specs = (P("dp", "factor"), P("dp", "factor"), P("factor", "dp"))
    return jax.shard_map(
        functools.partial(dispatch, mesh.shape["dp"], mesh.shape["factor"]), mesh=mesh, in_specs=in_specs, out_specs=out_specs, check_vma=False
    )
```
